32 devices in a mesh: seq: 16 (over z, y, core), rep: 2 (over x).
Axes of the slice: x: 2, y: 2, z: 4, core: 2. Of those that a mesh axis runs over, the one named last changes fastest.
Arguments:
- queries: bfloat16 [4096, 2048], P(('seq', 'rep')), may hold values from -128 to 128
- key_rows: bfloat16 [4096, 2048], P(('seq', 'rep')), may hold values from -4.5 to 4.5
- value_rows: bfloat16 [4096, 2048], P(('seq', 'rep')), may hold values from -6 to 6
- saved_output: bfloat16 [4096, 2048], P(('seq', 'rep')), may hold values from -6 to 6
- grad_output: bfloat16 [4096, 2048], P(('seq', 'rep')), may hold values from -6 to 6
- doc_lengths: int32 [16], replicated, may hold values from 1 to 1536, 4096 in all
Outputs:
- grad_query: bfloat16 [4096, 2048], P(('seq', 'rep'))
- grad_key: bfloat16 [4096, 2048], P(('seq', 'rep'))
- grad_value: bfloat16 [4096, 2048], P(('seq', 'rep'))
The draws below stay inside these ranges and needn't reach their ends.
Inputs may be any that keep to these rules, and one draw needn't show every extreme that they name: `doc_lengths`: documents in sequence order; they sum to 4096 and the longest has exactly 1536 tokens.
All inputs are finite; a program needn't handle non-finite values.
Results may differ from the reference program's by a relative error of at most 0.014.
Values may be sent and summed in bfloat16 or wider, within the bound.
A program may use at most 128 MiB of HBM per device.

```python
import math
import jax
import jax.numpy as jnp
import numpy as np
from jax import lax

HEAD_DIM = 128
HEADS = 16
TILE = 512
BAND = 512
SPAN = 2048
TOKENS = 4096
MAXDOC = 1536
NDOCS = 16


def drawn_keys(key):
    base = jax.random.truncated_normal(jax.random.fold_in(key, 11), -4.0, 4.0, (TOKENS, HEADS * HEAD_DIM), jnp.float32)
    return base


def draw_key_rows(key, part):
    return drawn_keys(key).astype(jnp.bfloat16)


def draw_queries(key, part):
    base = jax.random.truncated_normal(jax.random.fold_in(key, 23), -4.0, 4.0, (TOKENS, HEADS * HEAD_DIM), jnp.float32)
    return base.astype(jnp.bfloat16)


def levels(stream_key, shape, shards, low, top_value):
    factor_of, own = 1.0, jax.random.fold_in(stream_key, 6)
    for axis_at, shards_of in shards:
        draws = jnp.exp(jax.random.uniform(jax.random.fold_in(own, axis_at), (shards_of,), jnp.float32, low / len(shards), top_value / len(shards)))
        factor_of = factor_of * jnp.repeat(draws, shape[axis_at] // shards_of).reshape([-1 if axis == axis_at else 1 for axis in range(len(shape))])
    return factor_of


def split_up(number_of, total, most, lean):
    portions = [(1 << 20) // math.isqrt(grade ** lean) + 1 for grade in range(2, number_of + 1)]
    rest, counts = total - most - (number_of - 1), [1] * (number_of - 1)
    while rest > 0:
        movable = [i for i in range(number_of - 1) if counts[i] < most]
        whole, left = sum([portions[i] for i in movable]), rest
        for i in movable:
            more = min(most - counts[i], max(1, left * portions[i] // whole), rest)
            counts[i] = counts[i] + more
            rest = rest - more
    return np.array([most] + counts)


def uneven(stream_key, amount, total, limit, slope):
    if amount == 2:
        one = jax.random.randint(stream_key, (), max(1, total - limit), min(limit, total - 1) + 1)
        return jnp.stack([one, total - one])
    tallies = jnp.asarray(split_up(amount, total, limit, slope), jnp.int32)
    couples = (amount - 1) // 2
    giver, sink = tallies[1:1 + 2 * couples:2], tallies[2:2 + 2 * couples:2]
    slack = jnp.minimum(giver - 1, limit - sink)
    moved = jax.random.randint(jax.random.fold_in(stream_key, 1), (couples,), 0, 1 << 20) % (slack + 1)
    tallies = tallies.at[1:1 + 2 * couples:2].set(giver - moved).at[2:2 + 2 * couples:2].set(sink + moved)
    return tallies[jax.random.permutation(jax.random.fold_in(stream_key, 2), amount)]


def gaussian(stream_key, dims, width, reach, shards=(), kind=jnp.bfloat16):
    gain = levels(stream_key, dims, shards, -0.22, 0.18) if shards else 1.0
    result = jax.random.normal(stream_key, dims, jnp.float32) * width * gain
    return jnp.minimum(jnp.maximum(result, -reach), reach).astype(kind)


def setup_inputs(seed: int = 0) -> dict:
    splits = jax.random.split(jax.random.key(seed), 7)
    queries = draw_queries(jax.random.fold_in(splits[6], 71), 0)
    key_rows = draw_key_rows(jax.random.fold_in(splits[6], 71), 0)
    value_rows = gaussian(splits[2], (TOKENS, HEADS * HEAD_DIM), 1.0, 6.0, ((0, 32),))
    saved_output = gaussian(splits[3], (TOKENS, HEADS * HEAD_DIM), 1.0, 6.0, ((0, 32),))
    grad_output = gaussian(splits[4], (TOKENS, HEADS * HEAD_DIM), 1.0, 6.0, ((0, 32),))
    doc_lengths = uneven(splits[5], NDOCS, TOKENS, MAXDOC, 2).astype(jnp.int32)
    return {"queries": queries, "key_rows": key_rows, "value_rows": value_rows, "saved_output": saved_output, "grad_output": grad_output, "doc_lengths": doc_lengths}


NEG_FILL = -1.0e30


def reference(queries, key_rows, value_rows, saved_output, grad_output, doc_lengths):
    softmax_scale = HEAD_DIM ** -0.5
    window = SPAN
    margin = window - TILE

    def heads_of(array):
        return array.reshape(TOKENS, HEADS, HEAD_DIM)

    def padded(array):
        return jnp.concatenate([jnp.zeros((margin, HEADS, HEAD_DIM), array.dtype), heads_of(array)], axis=0)

    query_heads = heads_of(queries)
    dout_heads = heads_of(grad_output)
    output_heads = heads_of(saved_output)
    key_pad = padded(key_rows)
    value_pad = padded(value_rows)
    doc_ends = jnp.cumsum(doc_lengths).astype(jnp.int32)

    def step(grad_bufs, tile_id):
        dk_pad, dv_pad = grad_bufs
        row0 = (tile_id * TILE).astype(jnp.int32)
        row_ids = row0 + lax.iota(jnp.int32, TILE)
        col_ids = row0 + TILE - window + lax.iota(jnp.int32, window)
        before = jnp.sum(jnp.where(doc_ends[None, :] <= row_ids[:, None], doc_lengths[None, :], 0), axis=1)
        low_key = jnp.minimum(before, row_ids - BAND + 1)
        allowed = (col_ids[None, :] <= row_ids[:, None]) & (col_ids[None, :] >= low_key[:, None]) & (col_ids[None, :] >= 0)
        query_tile = lax.dynamic_slice_in_dim(query_heads, row0, TILE, 0).astype(jnp.float32)
        dout_tile = lax.dynamic_slice_in_dim(dout_heads, row0, TILE, 0).astype(jnp.float32)
        output_tile = lax.dynamic_slice_in_dim(output_heads, row0, TILE, 0).astype(jnp.float32)
        key_tile = lax.dynamic_slice_in_dim(key_pad, row0, window, 0).astype(jnp.float32)
        value_tile = lax.dynamic_slice_in_dim(value_pad, row0, window, 0).astype(jnp.float32)
        scores = jnp.einsum("thd,khd->htk", query_tile, key_tile) * softmax_scale
        masked = jnp.where(allowed[None], scores, NEG_FILL)
        row_max = jnp.max(masked, axis=-1)
        row_sum = jnp.sum(jnp.where(allowed[None], jnp.exp(masked - row_max[..., None]), 0.0), axis=-1)
        log_norm = row_max + jnp.log(row_sum)
        weights = jnp.where(allowed[None], jnp.exp(scores - log_norm[..., None]), 0.0)
        weights_low = lax.optimization_barrier(weights.astype(jnp.bfloat16)).astype(jnp.float32)
        row_delta = jnp.einsum("thd,thd->ht", dout_tile, output_tile)
        grad_weights = jnp.einsum("thd,khd->htk", dout_tile, value_tile)
        dscore = lax.optimization_barrier((weights * (grad_weights - row_delta[..., None])).astype(jnp.bfloat16)).astype(jnp.float32)
        grad_q = jnp.einsum("htk,khd->thd", dscore, key_tile) * softmax_scale
        dk_add = jnp.einsum("htk,thd->khd", dscore, query_tile)
        dv_add = jnp.einsum("htk,thd->khd", weights_low, dout_tile)
        dk_pad = lax.dynamic_update_slice_in_dim(dk_pad, lax.dynamic_slice_in_dim(dk_pad, row0, window, 0) + dk_add, row0, 0)
        dv_pad = lax.dynamic_update_slice_in_dim(dv_pad, lax.dynamic_slice_in_dim(dv_pad, row0, window, 0) + dv_add, row0, 0)
        return (dk_pad, dv_pad), grad_q.astype(jnp.bfloat16)

    start_bufs = (jnp.zeros((margin + TOKENS, HEADS, HEAD_DIM), jnp.float32), jnp.zeros((margin + TOKENS, HEADS, HEAD_DIM), jnp.float32))
    (dk_pad, dv_pad), dq_tiles = lax.scan(step, start_bufs, jnp.arange(TOKENS // TILE, dtype=jnp.int32))
    grad_query = dq_tiles.reshape(TOKENS, HEADS * HEAD_DIM)
    grad_key = (dk_pad[margin:] * softmax_scale).astype(jnp.bfloat16).reshape(TOKENS, HEADS * HEAD_DIM)
    grad_value = dv_pad[margin:].astype(jnp.bfloat16).reshape(TOKENS, HEADS * HEAD_DIM)
    return grad_query, grad_key, grad_value
```

```python
import functools

import jax
import jax.numpy as jnp
from jax import lax
from jax.experimental import pallas as pl
from jax.experimental.pallas import tpu as pltpu
from jax.sharding import PartitionSpec as P

HEAD_DIM = 128
TILE = 512
BAND = 512
CHUNK = 256
PAIR = 2
NEG_FILL = -1e30
SCALE = HEAD_DIM ** (-0.5)
MESH = pl.DeviceIdType.MESH
NT = (((1,), (1,)), ((), ()))
NN = (((1,), (0,)), ((), ()))
TN = (((0,), (0,)), ((), ()))


def greet(groups, helpers, me, rep):
    barrier = pltpu.get_barrier_semaphore()

    def to_group(step, carry):
        pl.semaphore_signal(
            barrier, inc=1, device_id=(lax.rem(me + step, groups), rep), device_id_type=MESH
        )
        return carry

    lax.fori_loop(1, groups, to_group, 0)
    for step in range(1, helpers):
        pl.semaphore_signal(
            barrier, inc=1, device_id=(me, lax.rem(rep + step, helpers)), device_id_type=MESH
        )
    pl.semaphore_wait(barrier, groups - 1 + helpers - 1)


def spread_kernel(
    groups,
    helpers,
    q_ref,
    k_ref,
    v_ref,
    o_ref,
    do_ref,
    qr,
    kr,
    vr,
    dor,
    dlr,
    delta,
    send_sem,
    recv_sem,
    fsend_sem,
    frecv_sem,
    own_sem,
):
    me = lax.axis_index("seq")
    rep = lax.axis_index("rep")
    greet(groups, helpers, me, rep)

    def columns(ref, head):
        return ref.at[:, pl.ds(pl.multiple_of(head * HEAD_DIM, HEAD_DIM), HEAD_DIM)]

    pairs = (
        (k_ref, lambda s: kr.at[s, rep]),
        (v_ref, lambda s: vr.at[s, rep]),
        (q_ref, lambda s: qr.at[s]),
        (do_ref, lambda s: dor.at[s]),
    )

    def outgoing(which, step):
        to = lax.rem(me + step, groups)
        src, dst = pairs[which]
        return pltpu.make_async_remote_copy(
            src_ref=columns(src, to),
            dst_ref=dst(me),
            send_sem=send_sem.at[which, step],
            recv_sem=recv_sem.at[which, step],
            device_id=(to, rep),
            device_id_type=MESH,
        )

    def arriving(which, step):
        source = lax.rem(me + groups - step, groups)
        src, dst = pairs[which]
        return pltpu.make_async_remote_copy(
            src_ref=columns(src, source),
            dst_ref=dst(source),
            send_sem=send_sem.at[which, step],
            recv_sem=recv_sem.at[which, step],
            device_id=(source, rep),
            device_id_type=MESH,
        )

    def own(which):
        src, dst = pairs[which]
        return pltpu.make_async_copy(columns(src, me), dst(me), own_sem.at[which])

    def forward(which, source, hop):
        dst = pairs[which][1]
        return pltpu.make_async_remote_copy(
            src_ref=dst(source),
            dst_ref=dst(source),
            send_sem=fsend_sem.at[which, hop - 1, source],
            recv_sem=frecv_sem.at[which, hop - 1, source],
            device_id=(me, lax.rem(rep + hop, helpers)),
            device_id_type=MESH,
        )

    def forwarded(which, source, hop):
        other = lax.rem(rep + helpers - hop, helpers)
        ref = (kr, vr)[which].at[source, other]
        return pltpu.make_async_remote_copy(
            src_ref=ref,
            dst_ref=ref,
            send_sem=fsend_sem.at[which, hop - 1, source],
            recv_sem=frecv_sem.at[which, hop - 1, source],
            device_id=(me, other),
            device_id_type=MESH,
        )

    for which in range(4):
        own(which).start()

        def send(step, carry, which=which):
            outgoing(which, step).start()
            return carry

        lax.fori_loop(1, groups, send, 0)

    def head_delta(head, carry):
        cols = pl.ds(pl.multiple_of(head * HEAD_DIM, HEAD_DIM), HEAD_DIM)
        prod = do_ref[:, cols].astype(jnp.float32) * o_ref[:, cols].astype(jnp.float32)
        row = jnp.sum(prod.T, axis=0, keepdims=True)
        delta[head] = jnp.broadcast_to(row, delta.shape[1:])
        return carry

    lax.fori_loop(0, groups, head_delta, 0)

    def delta_out(step):
        to = lax.rem(me + step, groups)
        return pltpu.make_async_remote_copy(
            src_ref=delta.at[to],
            dst_ref=dlr.at[me],
            send_sem=send_sem.at[4, step],
            recv_sem=recv_sem.at[4, step],
            device_id=(to, rep),
            device_id_type=MESH,
        )

    def delta_in(step):
        source = lax.rem(me + groups - step, groups)
        return pltpu.make_async_remote_copy(
            src_ref=delta.at[source],
            dst_ref=dlr.at[source],
            send_sem=send_sem.at[4, step],
            recv_sem=recv_sem.at[4, step],
            device_id=(source, rep),
            device_id_type=MESH,
        )

    own_delta = pltpu.make_async_copy(delta.at[me], dlr.at[me], own_sem.at[4])
    own_delta.start()

    def send_delta(step, carry):
        delta_out(step).start()
        return carry

    lax.fori_loop(1, groups, send_delta, 0)

    for which in range(2):
        own(which).wait()
        for hop in range(1, helpers):
            forward(which, me, hop).start()

        def relay(step, carry, which=which):
            arriving(which, step).wait_recv()
            for hop in range(1, helpers):
                forward(which, lax.rem(me + groups - step, groups), hop).start()
            return carry

        lax.fori_loop(1, groups, relay, 0)
    for which in range(2, 4):
        own(which).wait()

        def take(step, carry, which=which):
            arriving(which, step).wait_recv()
            return carry

        lax.fori_loop(1, groups, take, 0)

    own_delta.wait()

    def finish(step, carry):
        delta_in(step).wait_recv()
        delta_out(step).wait_send()
        for which in range(4):
            outgoing(which, step).wait_send()
        return carry

    lax.fori_loop(1, groups, finish, 0)

    def finish_forward(source, carry):
        for which in range(2):
            for hop in range(1, helpers):
                forwarded(which, source, hop).wait_recv()
                forward(which, source, hop).wait_send()
        return carry

    lax.fori_loop(0, groups, finish_forward, 0)


def attend_kernel(
    groups,
    helpers,
    tok,
    docs_ref,
    q_ref,
    k_ref,
    v_ref,
    do_ref,
    dl_ref,
    dq_ref,
    dk_ref,
    dv_ref,
    s_ref,
    dk_acc,
    dv_acc,
):
    rep = lax.axis_index("rep")
    total = groups * helpers * tok
    width = PAIR * tok
    docs = docs_ref.shape[0]

    def clear(c, carry):
        rows = pl.ds(pl.multiple_of(c * CHUNK, CHUNK), CHUNK)
        dk_acc[rows, :] = jnp.zeros((CHUNK, HEAD_DIM), jnp.float32)
        dv_acc[rows, :] = jnp.zeros((CHUNK, HEAD_DIM), jnp.float32)
        return carry

    lax.fori_loop(0, total // CHUNK, clear, 0)

    def tile(t, carry):
        lane = lax.broadcasted_iota(jnp.int32, (1, width), 1)
        row = ((t * PAIR + lane // tok) * helpers + rep) * tok + lane % tok
        first = (t * PAIR * helpers + rep) * tok
        last = ((t * PAIR + PAIR - 1) * helpers + rep) * tok + tok - 1

        def per_doc(d, state):
            end, start, starts = state
            end = end + docs_ref[d]
            return (
                end,
                jnp.where(end <= first, end, start),
                jnp.where(end <= row, end, starts),
            )

        unused, start, starts = lax.fori_loop(
            0, docs, per_doc, (jnp.int32(0), jnp.int32(0), jnp.zeros((1, width), jnp.int32))
        )
        low = jnp.minimum(starts, row - (BAND - 1))
        lo = jnp.maximum(jnp.minimum(start, first - (BAND - 1)), 0) // CHUNK
        hi = last // CHUNK + 1
        mine = pl.ds(pl.multiple_of(t * width, width), width)
        queries = q_ref[mine, :]
        douts = do_ref[mine, :]

        def stat(c, state):
            top, norm = state
            keys = k_ref[pl.ds(pl.multiple_of(c * CHUNK, CHUNK), CHUNK), :]
            scores = lax.dot_general(keys, queries, NT, preferred_element_type=jnp.float32) * SCALE
            kid = lax.broadcasted_iota(jnp.int32, (CHUNK, width), 0)
            base = c * CHUNK
            allowed = (kid <= row - base) & (kid >= low - base)
            scores = jnp.where(allowed, scores, NEG_FILL)
            s_ref[pl.ds(pl.multiple_of((c - lo) * CHUNK, CHUNK), CHUNK), :] = scores
            new_top = jnp.maximum(top, jnp.max(scores, axis=0, keepdims=True))
            fresh = jnp.sum(jnp.exp(scores - new_top), axis=0, keepdims=True)
            return new_top, norm * jnp.exp(top - new_top) + fresh

        top, norm = lax.fori_loop(
            lo,
            hi,
            stat,
            (jnp.full((1, width), NEG_FILL, jnp.float32), jnp.zeros((1, width), jnp.float32)),
        )
        log_norm = top + jnp.log(norm)
        delta = jnp.concatenate([dl_ref[t * PAIR + i, 0:1, :] for i in range(PAIR)], axis=1)

        def grad(c, dq):
            rows = pl.ds(pl.multiple_of(c * CHUNK, CHUNK), CHUNK)
            scores = s_ref[pl.ds(pl.multiple_of((c - lo) * CHUNK, CHUNK), CHUNK), :]
            weights = jnp.exp(scores - log_norm)
            grad_weights = lax.dot_general(
                v_ref[rows, :], douts, NT, preferred_element_type=jnp.float32
            )
            dscore = (weights * (grad_weights - delta)).astype(jnp.bfloat16)
            dv_acc[rows, :] += lax.dot_general(
                weights.astype(jnp.bfloat16), douts, NN, preferred_element_type=jnp.float32
            )
            dk_acc[rows, :] += lax.dot_general(
                dscore, queries, NN, preferred_element_type=jnp.float32
            )
            return dq + lax.dot_general(
                k_ref[rows, :], dscore, TN, preferred_element_type=jnp.float32
            )

        dq = lax.fori_loop(lo, hi, grad, jnp.zeros((HEAD_DIM, width), jnp.float32))
        dq_ref[mine, :] = (dq.T * SCALE).astype(jnp.bfloat16)
        return carry

    lax.fori_loop(0, groups // PAIR, tile, 0)

    def settle(c, carry):
        rows = pl.ds(pl.multiple_of(c * CHUNK, CHUNK), CHUNK)
        dk_ref[rows, :] = (dk_acc[rows, :] * SCALE).astype(jnp.bfloat16)
        dv_ref[rows, :] = dv_acc[rows, :].astype(jnp.bfloat16)
        return carry

    lax.fori_loop(0, total // CHUNK, settle, 0)


def gather_kernel(
    groups,
    helpers,
    dq_ref,
    dk_ref,
    dv_ref,
    gq,
    gk,
    gv,
    part,
    summed,
    send_sem,
    recv_sem,
    psend_sem,
    precv_sem,
    own_sem,
):
    me = lax.axis_index("seq")
    rep = lax.axis_index("rep")
    greet(groups, helpers, me, rep)
    partials = (dk_ref, dv_ref)
    results = (gk, gv, gq)

    def columns(ref, head):
        return ref.at[:, pl.ds(pl.multiple_of(head * HEAD_DIM, HEAD_DIM), HEAD_DIM)]

    def share(which, step, hop):
        to_rep = lax.rem(rep + hop, helpers)
        block = lax.rem(me + step, groups)
        return pltpu.make_async_remote_copy(
            src_ref=partials[which].at[block, to_rep],
            dst_ref=part.at[which, hop - 1, block],
            send_sem=psend_sem.at[which, hop - 1, step],
            recv_sem=precv_sem.at[which, hop - 1, step],
            device_id=(me, to_rep),
            device_id_type=MESH,
        )

    def source_of(which, block):
        return dq_ref.at[block] if which == 2 else summed.at[which, block]

    def home(which, step):
        to = lax.rem(me + step, groups)
        return pltpu.make_async_remote_copy(
            src_ref=source_of(which, to),
            dst_ref=columns(results[which], me),
            send_sem=send_sem.at[which, step],
            recv_sem=recv_sem.at[which, step],
            device_id=(to, rep),
            device_id_type=MESH,
        )

    def came(which, step):
        source = lax.rem(me + groups - step, groups)
        return pltpu.make_async_remote_copy(
            src_ref=source_of(which, source),
            dst_ref=columns(results[which], source),
            send_sem=send_sem.at[which, step],
            recv_sem=recv_sem.at[which, step],
            device_id=(source, rep),
            device_id_type=MESH,
        )

    def own(which):
        return pltpu.make_async_copy(
            source_of(which, me), columns(results[which], me), own_sem.at[which]
        )

    for which in range(2):

        def start_share(step, carry, which=which):
            for hop in range(1, helpers):
                share(which, step, hop).start()
            return carry

        lax.fori_loop(0, groups, start_share, 0)

    def start_query(step, carry):
        home(2, step).start()
        return carry

    lax.fori_loop(1, groups, start_query, 0)
    own(2).start()

    def add(which, step):
        block = lax.rem(me + step, groups)
        value = partials[which][block, rep].astype(jnp.float32)
        for hop in range(1, helpers):
            share(which, step, hop).wait_recv()
            value = value + part[which, hop - 1, block].astype(jnp.float32)
        summed[which, block] = value.astype(jnp.bfloat16)

    for which in range(2):

        def add_send(step, carry, which=which):
            add(which, step)
            home(which, step).start()
            return carry

        lax.fori_loop(1, groups, add_send, 0)
        add(which, 0)
        own(which).start()

    for which in range(3):
        own(which).wait()

    def finish(step, carry):
        for which in range(3):
            home(which, step).wait_send()
            came(which, step).wait_recv()
        return carry

    lax.fori_loop(1, groups, finish, 0)

    def finish_share(step, carry):
        for which in range(2):
            for hop in range(1, helpers):
                share(which, step, hop).wait_send()
        return carry

    lax.fori_loop(0, groups, finish_share, 0)


def shards(queries, key_rows, value_rows, saved_output, grad_output, doc_lengths):
    groups = lax.axis_size("seq")
    helpers = lax.axis_size("rep")
    tok = queries.shape[0]
    total = tok * groups * helpers
    longest = tok * groups - TILE
    low = jnp.bfloat16
    dma = pltpu.SemaphoreType.DMA
    anywhere = pl.BlockSpec(memory_space=pl.ANY)
    in_vmem = pl.BlockSpec(memory_space=pltpu.VMEM)
    block = (tok, HEAD_DIM)
    q, k, v, do, delta = pl.pallas_call(
        functools.partial(spread_kernel, groups, helpers),
        out_shape=(
            jax.ShapeDtypeStruct((groups, *block), low),
            jax.ShapeDtypeStruct((groups, helpers, *block), low),
            jax.ShapeDtypeStruct((groups, helpers, *block), low),
            jax.ShapeDtypeStruct((groups, *block), low),
            jax.ShapeDtypeStruct((groups, 8, tok), jnp.float32),
        ),
        in_specs=[anywhere, anywhere, anywhere, in_vmem, in_vmem],
        out_specs=[anywhere] * 5,
        scratch_shapes=[
            pltpu.VMEM((groups, 8, tok), jnp.float32),
            dma((5, groups)),
            dma((5, groups)),
            dma((2, helpers - 1, groups)),
            dma((2, helpers - 1, groups)),
            dma((5,)),
        ],
        compiler_params=pltpu.CompilerParams(
            collective_id=0, has_side_effects=True, vmem_limit_bytes=16 << 20
        ),
        name="spread",
    )(queries, key_rows, value_rows, saved_output, grad_output)

    reach = (PAIR - 1) * helpers * tok + tok + max(longest, BAND)
    window = min(total, (reach // CHUNK + 2) * CHUNK)
    dq, dk, dv = pl.pallas_call(
        functools.partial(attend_kernel, groups, helpers, tok),
        out_shape=(
            jax.ShapeDtypeStruct((groups * tok, HEAD_DIM), low),
            jax.ShapeDtypeStruct((total, HEAD_DIM), low),
            jax.ShapeDtypeStruct((total, HEAD_DIM), low),
        ),
        in_specs=[pl.BlockSpec(memory_space=pltpu.SMEM)] + [in_vmem] * 5,
        out_specs=[in_vmem] * 3,
        scratch_shapes=[
            pltpu.VMEM((window, PAIR * tok), jnp.float32),
            pltpu.VMEM((total, HEAD_DIM), jnp.float32),
            pltpu.VMEM((total, HEAD_DIM), jnp.float32),
        ],
        compiler_params=pltpu.CompilerParams(vmem_limit_bytes=56 << 20),
        name="attend",
    )(
        doc_lengths,
        q.reshape(-1, HEAD_DIM),
        k.reshape(-1, HEAD_DIM),
        v.reshape(-1, HEAD_DIM),
        do.reshape(-1, HEAD_DIM),
        delta,
    )

    return pl.pallas_call(
        functools.partial(gather_kernel, groups, helpers),
        out_shape=(jax.ShapeDtypeStruct(queries.shape, low),) * 3,
        in_specs=[anywhere, in_vmem, in_vmem],
        out_specs=[anywhere] * 3,
        scratch_shapes=[
            pltpu.VMEM((2, helpers - 1, groups, *block), low),
            pltpu.VMEM((2, groups, *block), low),
            dma((3, groups)),
            dma((3, groups)),
            dma((2, helpers - 1, groups)),
            dma((2, helpers - 1, groups)),
            dma((3,)),
        ],
        compiler_params=pltpu.CompilerParams(
            collective_id=1, has_side_effects=True, vmem_limit_bytes=48 << 20
        ),
        name="gather",
    )(
        dq.reshape(groups, *block),
        dk.reshape(groups, helpers, *block),
        dv.reshape(groups, helpers, *block),
    )


def solution(mesh):
    tokens = P(("seq", "rep"), None)
    return jax.shard_map(
        shards,
        mesh=mesh,
        in_specs=(tokens,) * 5 + (P(),),
        out_specs=(tokens,) * 3,
        check_vma=False,
    )
```

```python
import functools

import jax
import jax.numpy as jnp
from jax import lax
from jax.experimental import pallas as pl
from jax.experimental.pallas import tpu as pltpu
from jax.sharding import PartitionSpec as P

HEAD_DIM = 128
TILE = 512
BAND = 512
CHUNK = 512
PAIR = 2
NEG_FILL = -1e30
SCALE = HEAD_DIM ** (-0.5)
MESH = pl.DeviceIdType.MESH
NT = (((1,), (1,)), ((), ()))
NN = (((1,), (0,)), ((), ()))
TN = (((0,), (0,)), ((), ()))


def greet(groups, helpers, me, rep):
    barrier = pltpu.get_barrier_semaphore()

    def to_group(step, carry):
        pl.semaphore_signal(
            barrier, inc=1, device_id=(lax.rem(me + step, groups), rep), device_id_type=MESH
        )
        return carry

    lax.fori_loop(1, groups, to_group, 0)
    for step in range(1, helpers):
        pl.semaphore_signal(
            barrier, inc=1, device_id=(me, lax.rem(rep + step, helpers)), device_id_type=MESH
        )
    pl.semaphore_wait(barrier, groups - 1 + helpers - 1)


def windows(groups, helpers, tok):
    longest = max(tok * groups - TILE, BAND)

    def of(t, rep):
        first = (t * PAIR * helpers + rep) * tok
        last = ((t * PAIR + PAIR - 1) * helpers + rep) * tok + tok - 1
        lo = first - (longest - 1)
        if isinstance(lo, int):
            return max(lo, 0) // CHUNK, last // CHUNK + 1
        return jnp.maximum(lo, 0) // CHUNK, last // CHUNK + 1

    most = 0
    for t in range(groups // PAIR):
        for rep in range(helpers):
            lo, hi = of(t, rep)
            most = max(most, hi - lo)
    return of, most


def fused_kernel(
    groups,
    helpers,
    tok,
    keep,
    docs_ref,
    q_ref,
    k_ref,
    v_ref,
    o_ref,
    do_ref,
    gq,
    gk,
    gv,
    qr,
    kr,
    vr,
    dor,
    dlr,
    delta,
    stats,
    kept,
    dk_acc,
    dv_acc,
    mine_part,
    part,
    summed,
    dqs,
    send_sem,
    recv_sem,
    fsend_sem,
    frecv_sem,
    own_sem,
    hsend_sem,
    hrecv_sem,
    psend_sem,
    precv_sem,
    hown_sem,
):
    me = lax.axis_index("seq")
    rep = lax.axis_index("rep")
    width = PAIR * tok
    tiles = groups // PAIR
    blocks = CHUNK // tok
    window, most = windows(groups, helpers, tok)
    greet(groups, helpers, me, rep)

    def columns(ref, head):
        return ref.at[:, pl.ds(pl.multiple_of(head * HEAD_DIM, HEAD_DIM), HEAD_DIM)]

    def flat(s, r):
        return s * helpers + r

    K, Q, DO, V, DELTA = range(5)
    pairs = (
        (lambda g: columns(k_ref, g), lambda s: kr.at[flat(s, rep)]),
        (lambda g: columns(q_ref, g), lambda s: qr.at[s]),
        (lambda g: columns(do_ref, g), lambda s: dor.at[s]),
        (lambda g: columns(v_ref, g), lambda s: vr.at[flat(s, rep)]),
        (lambda g: delta.at[g], lambda s: dlr.at[s]),
    )

    def outgoing(which, step):
        to = lax.rem(me + step, groups)
        src, dst = pairs[which]
        return pltpu.make_async_remote_copy(
            src_ref=src(to),
            dst_ref=dst(me),
            send_sem=send_sem.at[which, step],
            recv_sem=recv_sem.at[which, step],
            device_id=(to, rep),
            device_id_type=MESH,
        )

    def arriving(which, step):
        source = lax.rem(me + groups - step, groups)
        src, dst = pairs[which]
        return pltpu.make_async_remote_copy(
            src_ref=src(source),
            dst_ref=dst(source),
            send_sem=send_sem.at[which, step],
            recv_sem=recv_sem.at[which, step],
            device_id=(source, rep),
            device_id_type=MESH,
        )

    def own(which):
        src, dst = pairs[which]
        return pltpu.make_async_copy(src(me), dst(me), own_sem.at[which])

    def forward(which, source, hop):
        ref = pairs[which][1](source)
        return pltpu.make_async_remote_copy(
            src_ref=ref,
            dst_ref=ref,
            send_sem=fsend_sem.at[which // V, hop - 1, source],
            recv_sem=frecv_sem.at[which // V, hop - 1, source],
            device_id=(me, lax.rem(rep + hop, helpers)),
            device_id_type=MESH,
        )

    def forwarded(which, source, hop):
        other = lax.rem(rep + helpers - hop, helpers)
        ref = (kr if which == K else vr).at[flat(source, other)]
        return pltpu.make_async_remote_copy(
            src_ref=ref,
            dst_ref=ref,
            send_sem=fsend_sem.at[which // V, hop - 1, source],
            recv_sem=frecv_sem.at[which // V, hop - 1, source],
            device_id=(me, other),
            device_id_type=MESH,
        )

    def send_all(which):
        own(which).start()

        def send(step, carry):
            outgoing(which, step).start()
            return carry

        lax.fori_loop(1, groups, send, 0)

    def take_all(which):
        own(which).wait()

        def take(step, carry):
            arriving(which, step).wait_recv()
            return carry

        lax.fori_loop(1, groups, take, 0)

    def relay(which, step):
        arriving(which, step).wait_recv()
        for hop in range(1, helpers):
            forward(which, lax.rem(me + groups - step, groups), hop).start()

    def relay_own(which):
        own(which).wait()
        for hop in range(1, helpers):
            forward(which, me, hop).start()

    def take_forwarded(which):
        def take(source, carry):
            for hop in range(1, helpers):
                forwarded(which, source, hop).wait_recv()
            return carry

        lax.fori_loop(0, groups, take, 0)

    for which in (K, Q, DO, V):
        send_all(which)

    def head_delta(head, carry):
        cols = pl.ds(pl.multiple_of(head * HEAD_DIM, HEAD_DIM), HEAD_DIM)
        prod = do_ref[:, cols].astype(jnp.float32) * o_ref[:, cols].astype(jnp.float32)
        row = jnp.sum(prod.T, axis=0, keepdims=True)
        delta[head] = jnp.broadcast_to(row, delta.shape[1:])
        return carry

    lax.fori_loop(0, groups, head_delta, 0)
    send_all(DELTA)

    def clear(b, carry):
        dk_acc[b] = jnp.zeros((tok, HEAD_DIM), jnp.float32)
        dv_acc[b] = jnp.zeros((tok, HEAD_DIM), jnp.float32)
        return carry

    lax.fori_loop(0, groups * helpers, clear, 0)

    def relay_step(which):
        def run(step, carry):
            relay(which, step)
            return carry

        return run

    relay_own(K)
    lax.fori_loop(1, groups, relay_step(K), 0)
    take_all(Q)
    take_forwarded(K)

    def chunk_of(ref, c):
        return ref[pl.ds(c * blocks, blocks)].reshape(CHUNK, HEAD_DIM)

    def rows_of(ref, t):
        return ref[pl.ds(t * PAIR, PAIR)].reshape(width, HEAD_DIM)

    def limits(t):
        lane = lax.broadcasted_iota(jnp.int32, (1, width), 1)
        row = ((t * PAIR + lane // tok) * helpers + rep) * tok + lane % tok

        def per_doc(d, state):
            end, starts = state
            end = end + docs_ref[d]
            return end, jnp.where(end <= row, end, starts)

        unused, starts = lax.fori_loop(
            0, docs_ref.shape[0], per_doc, (jnp.int32(0), jnp.zeros((1, width), jnp.int32))
        )
        return row, jnp.minimum(starts, row - (BAND - 1))

    def scores_of(c, queries, row, low):
        scores = lax.dot_general(
            chunk_of(kr, c), queries, NT, preferred_element_type=jnp.float32
        )
        kid = lax.broadcasted_iota(jnp.int32, (CHUNK, width), 0)
        allowed = (kid <= row - c * CHUNK) & (kid >= low - c * CHUNK)
        return jnp.where(allowed, scores * SCALE, NEG_FILL)

    def stat_tile(t, carry):
        lo, hi = window(t, rep)
        row, low = limits(t)
        queries = rows_of(qr, t)

        def stat(c, state):
            top, norm = state
            scores = scores_of(c, queries, row, low)
            if keep:
                kept[t * most + c - lo] = scores
            new_top = jnp.maximum(top, jnp.max(scores, axis=0, keepdims=True))
            fresh = jnp.sum(jnp.exp(scores - new_top), axis=0, keepdims=True)
            return new_top, norm * jnp.exp(top - new_top) + fresh

        start = (jnp.full((1, width), NEG_FILL, jnp.float32), jnp.zeros((1, width), jnp.float32))
        top, norm = lax.fori_loop(lo, hi, stat, start)
        stats[t] = jnp.broadcast_to(top + jnp.log(norm), stats.shape[1:])
        return carry

    lax.fori_loop(0, tiles, stat_tile, 0)
    take_all(DO)
    take_all(DELTA)
    relay_own(V)

    def value_tile(t, carry):
        for i in range(PAIR):
            step = t * PAIR + i

            @pl.when(step > 0)
            def _():
                relay(V, step)

        lo, hi = window(t, rep)
        douts = rows_of(dor, t)
        log_norm = stats[t, 0:1, :]
        if not keep:
            row, low = limits(t)
            queries = rows_of(qr, t)

        def value(c, carry):
            if keep:
                weights = jnp.exp(kept[t * most + c - lo] - log_norm)
                kept[t * most + c - lo] = weights
            else:
                weights = jnp.exp(scores_of(c, queries, row, low) - log_norm)
            add = lax.dot_general(
                weights.astype(jnp.bfloat16), douts, NN, preferred_element_type=jnp.float32
            )
            dv_acc[pl.ds(c * blocks, blocks)] += add.reshape(blocks, tok, HEAD_DIM)
            return carry

        lax.fori_loop(lo, hi, value, 0)
        return carry

    lax.fori_loop(0, tiles, value_tile, 0)

    results = (gk, gv, gq)

    def share(which, step, hop):
        to_rep = lax.rem(rep + hop, helpers)
        block = lax.rem(me + step, groups)
        return pltpu.make_async_remote_copy(
            src_ref=mine_part.at[which, flat(block, to_rep)],
            dst_ref=part.at[which, hop - 1, block],
            send_sem=psend_sem.at[which, hop - 1, step],
            recv_sem=precv_sem.at[which, hop - 1, step],
            device_id=(me, to_rep),
            device_id_type=MESH,
        )

    def source_of(which, block):
        return dqs.at[block] if which == 2 else summed.at[which, block]

    def home(which, step):
        to = lax.rem(me + step, groups)
        return pltpu.make_async_remote_copy(
            src_ref=source_of(which, to),
            dst_ref=columns(results[which], me),
            send_sem=hsend_sem.at[which, step],
            recv_sem=hrecv_sem.at[which, step],
            device_id=(to, rep),
            device_id_type=MESH,
        )

    def came(which, step):
        source = lax.rem(me + groups - step, groups)
        return pltpu.make_async_remote_copy(
            src_ref=source_of(which, source),
            dst_ref=columns(results[which], source),
            send_sem=hsend_sem.at[which, step],
            recv_sem=hrecv_sem.at[which, step],
            device_id=(source, rep),
            device_id_type=MESH,
        )

    def own_home(which):
        return pltpu.make_async_copy(
            source_of(which, me), columns(results[which], me), hown_sem.at[which]
        )

    accs = (dk_acc, dv_acc)
    factors = (SCALE, 1.0)

    def share_all(which):
        def run(step, carry):
            block = lax.rem(me + step, groups)
            for hop in range(1, helpers):
                at = flat(block, lax.rem(rep + hop, helpers))
                mine_part[which, at] = (accs[which][at] * factors[which]).astype(jnp.bfloat16)
                share(which, step, hop).start()
            return carry

        lax.fori_loop(0, groups, run, 0)

    def add(which, step):
        block = lax.rem(me + step, groups)
        value = accs[which][flat(block, rep)] * factors[which]
        for hop in range(1, helpers):
            share(which, step, hop).wait_recv()
            value = value + part[which, hop - 1, block].astype(jnp.float32)
        summed[which, block] = value.astype(jnp.bfloat16)

    def add_all(which):
        def run(step, carry):
            add(which, step)
            home(which, step).start()
            return carry

        add(which, 0)
        own_home(which).start()
        lax.fori_loop(1, groups, run, 0)

    share_all(1)
    take_forwarded(V)

    def grad_tile(turn, carry):
        t = lax.rem(turn + me // PAIR + 1, tiles)
        lo, hi = window(t, rep)
        queries = rows_of(qr, t)
        douts = rows_of(dor, t)
        log_norm = stats[t, 0:1, :]
        shift = jnp.concatenate([dlr[t * PAIR + i, 0:1, :] for i in range(PAIR)], axis=1)
        if not keep:
            row, low = limits(t)

        def grad(c, dq):
            if keep:
                weights = kept[t * most + c - lo]
            else:
                weights = jnp.exp(scores_of(c, queries, row, low) - log_norm)
            grad_weights = lax.dot_general(
                chunk_of(vr, c), douts, NT, preferred_element_type=jnp.float32
            )
            dscore = (weights * (grad_weights - shift)).astype(jnp.bfloat16)
            add = lax.dot_general(dscore, queries, NN, preferred_element_type=jnp.float32)
            dk_acc[pl.ds(c * blocks, blocks)] += add.reshape(blocks, tok, HEAD_DIM)
            return dq + lax.dot_general(
                chunk_of(kr, c), dscore, TN, preferred_element_type=jnp.float32
            )

        dq = lax.fori_loop(lo, hi, grad, jnp.zeros((HEAD_DIM, width), jnp.float32))
        rows = (dq.T * SCALE).astype(jnp.bfloat16)
        dqs[pl.ds(t * PAIR, PAIR)] = rows.reshape(PAIR, tok, HEAD_DIM)
        for i in range(PAIR):
            block = t * PAIR + i
            step = lax.rem(block + groups - me, groups)

            @pl.when(step > 0)
            def _():
                home(2, step).start()

        return carry

    lax.fori_loop(0, tiles // 2, grad_tile, 0)
    add_all(1)
    lax.fori_loop(tiles // 2, tiles, grad_tile, 0)
    share_all(0)
    own_home(2).start()
    add_all(0)

    for which in range(3):
        own_home(which).wait()

    def finish(step, carry):
        for which in range(5):
            outgoing(which, step).wait_send()
        for which in range(3):
            home(which, step).wait_send()
            came(which, step).wait_recv()
        return carry

    lax.fori_loop(1, groups, finish, 0)

    def finish_rep(step, carry):
        for hop in range(1, helpers):
            for which in (K, V):
                forward(which, step, hop).wait_send()
            for which in range(2):
                share(which, step, hop).wait_send()
        return carry

    lax.fori_loop(0, groups, finish_rep, 0)


def shards(queries, key_rows, value_rows, saved_output, grad_output, doc_lengths):
    groups = lax.axis_size("seq")
    helpers = lax.axis_size("rep")
    tok = queries.shape[0]
    everything = groups * helpers
    tiles = groups // PAIR
    low = jnp.bfloat16
    dma = pltpu.SemaphoreType.DMA
    vmem = pltpu.VMEM
    anywhere = pl.BlockSpec(memory_space=pl.ANY)
    in_vmem = pl.BlockSpec(memory_space=pltpu.VMEM)
    block = (tok, HEAD_DIM)
    unused, most = windows(groups, helpers, tok)
    slots = tiles * most
    keep = slots * CHUNK * PAIR * tok * 4 <= 24 << 20
    return pl.pallas_call(
        functools.partial(fused_kernel, groups, helpers, tok, keep),
        out_shape=(jax.ShapeDtypeStruct(queries.shape, low),) * 3,
        in_specs=[
            pl.BlockSpec(memory_space=pltpu.SMEM),
            anywhere,
            anywhere,
            anywhere,
            in_vmem,
            in_vmem,
        ],
        out_specs=[anywhere] * 3,
        scratch_shapes=[
            vmem((groups, *block), low),
            vmem((everything, *block), low),
            vmem((everything, *block), low),
            vmem((groups, *block), low),
            vmem((groups, 8, tok), jnp.float32),
            vmem((groups, 8, tok), jnp.float32),
            vmem((tiles, 8, PAIR * tok), jnp.float32),
            vmem((slots if keep else 1, CHUNK, PAIR * tok), jnp.float32),
            vmem((everything, *block), jnp.float32),
            vmem((everything, *block), jnp.float32),
            vmem((2, everything, *block), low),
            vmem((2, helpers - 1, groups, *block), low),
            vmem((2, groups, *block), low),
            vmem((groups, *block), low),
            dma((5, groups)),
            dma((5, groups)),
            dma((2, helpers - 1, groups)),
            dma((2, helpers - 1, groups)),
            dma((5,)),
            dma((3, groups)),
            dma((3, groups)),
            dma((2, helpers - 1, groups)),
            dma((2, helpers - 1, groups)),
            dma((3,)),
        ],
        compiler_params=pltpu.CompilerParams(
            collective_id=0, has_side_effects=True, vmem_limit_bytes=60 << 20
        ),
        name="fused",
    )(doc_lengths, queries, key_rows, value_rows, saved_output, grad_output)


def solution(mesh):
    tokens = P(("seq", "rep"), None)
    return jax.shard_map(
        shards,
        mesh=mesh,
        in_specs=(tokens,) * 5 + (P(),),
        out_specs=(tokens,) * 3,
        check_vma=False,
    )
```
